32 devices in a mesh: section: 2 (over core), row: 4 (over y, x), col: 4 (over z).
Axes of the slice: x: 2, y: 2, z: 4, core: 2. Of those that a mesh axis runs over, the one named last changes fastest.
Arguments:
- coeffs: bfloat16 [2, 4096, 6144], P('section', 'row', 'col'), may hold values from -0.21875 to 0.21875
- occ_energy: float32 [2], P('section'), may hold values from -1 to -0.3
- vir_energy: float32 [4096], P('row'), may hold values from 0.1 to 4
- frequency: float32 [], replicated, may hold values from 0.3 to 3
Outputs:
- response: float32 [6144, 6144], P(('section', 'row'), 'col')
The draws below stay inside these ranges and needn't reach their ends.
All inputs are finite; a program needn't handle non-finite values.
Results may differ from the reference program's by a relative error of at most 0.0012.
Values may be sent and summed in bfloat16 or wider, within the bound.
A program may use at most 128 MiB of HBM per device.

```python
import math
import jax
import jax.numpy as jnp
from jax import lax

NAUX = 6144
NVIR = 4096
NOCC = 2


def strengthened(array, own_key, source, target, parts, factor):
    def block_of(axis_at):
        return (jnp.arange(array.shape[axis_at]) // (array.shape[axis_at] // parts)).reshape((-1,) + (1,) * (array.ndim - 1 - axis_at))

    near = jax.random.permutation(own_key, parts)[block_of(target)]
    second = (block_of(target) + parts // 2) % parts
    return jnp.where((block_of(source) == near) | (block_of(source) == second), factor * array, array)


def levels(stream_key, extent, split, low, high):
    gain, own = 1.0, jax.random.fold_in(stream_key, 6)
    for dim, blocks in split:
        draws = jnp.exp(jax.random.uniform(jax.random.fold_in(own, dim), (blocks,), jnp.float32, low / len(split), high / len(split)))
        gain = gain * jnp.repeat(draws, extent[dim] // blocks).reshape([-1 if axis == dim else 1 for axis in range(len(extent))])
    return gain


def bell_draw_with(rng, dims, deviation, reach, shards, heavy, kind=jnp.bfloat16):
    array = deviation * jax.random.normal(rng, dims, jnp.float32)
    if shards:
        array = array * levels(rng, dims, shards, -0.22, 0.18)
    return jnp.clip(strengthened(array, jax.random.fold_in(rng, 3), *heavy), -reach, reach).astype(kind)


def setup_inputs(seed: int = 0) -> dict:
    seeds = jax.random.split(jax.random.key(seed), 5)
    return {
        "coeffs": bell_draw_with(seeds[0], (NOCC, NVIR, NAUX), ((NOCC * NVIR) ** -0.5), 0.21875, ((0, 2), (1, 4), (2, 4)), (0, 2, 2, 2.0)),
        "occ_energy": jnp.clip(-1.0 + 0.7 * jax.random.uniform(seeds[1], (NOCC,), jnp.float32) ** levels(seeds[1], (NOCC,), ((0, 2),), -0.2, 0.2), -1.0, -0.3),
        "vir_energy": jnp.clip(jnp.exp(math.log(4.0) - 3.6888794 * jax.random.uniform(seeds[2], (NVIR,), jnp.float32) ** levels(seeds[2], (NVIR,), ((0, 4),), -0.2, 0.2)), 0.1, 4.0),
        "frequency": jnp.clip(jnp.exp(jax.random.uniform(seeds[3], (), jnp.float32, math.log(0.3), math.log(3.0))), 0.3, 3.0),
    }


def reference(coeffs, occ_energy, vir_energy, frequency):
    def add_orbital(running, inputs):
        orbital_rows, energy = inputs
        energy_gap = vir_energy - energy
        factor = 2.0 * energy_gap / (energy_gap * energy_gap + frequency * frequency)
        scaled = (orbital_rows.astype(jnp.float32) * factor[:, None]).astype(jnp.bfloat16)
        running = running + jnp.dot(scaled.astype(jnp.float32).T, orbital_rows.astype(jnp.float32), precision=lax.Precision.HIGHEST)
        return running, None

    start_sum = jnp.zeros((NAUX, NAUX), jnp.float32)
    running, unused = lax.scan(add_orbital, start_sum, (coeffs, occ_energy))
    return running
```

```python
import functools

import jax
import jax.numpy as jnp
from jax import lax
from jax.experimental import pallas as pl
from jax.experimental.pallas import tpu as pltpu
from jax.sharding import PartitionSpec as P

MESH = pl.DeviceIdType.MESH


def response_kernel(S, R, C, packed, coeffs, out, pbuf, qbuf, tiles, parts, loc_sem, p_send, p_recv, a_send, q_send, q_recv, f_send, f_recv, y_send, y_recv):
    width, depth = packed.shape[1], packed.shape[2]
    columns = coeffs.shape[1]
    blocks = S * R // C
    shares = R // blocks
    step = columns // 3 if columns % 384 == 0 else columns
    s = lax.axis_index("section")
    r = lax.axis_index("row")
    z = lax.axis_index("col")
    share, half = r // blocks, r % blocks
    right, left = (z + 1) % C, (z + C - 1) % C

    def peer(j):
        total, unit = 0, 1
        while unit < R:
            total = total + ((r // unit + j // unit) % 2) * unit
            unit *= 2
        return total

    barrier = pltpu.get_barrier_semaphore()
    for j in range(1, R):
        pl.semaphore_signal(barrier, inc=1, device_id={"row": peer(j)}, device_id_type=MESH)
    for other in (left, right):
        pl.semaphore_signal(barrier, inc=1, device_id={"col": other}, device_id_type=MESH)
    for i in range(1, S):
        pl.semaphore_signal(barrier, inc=1, device_id={"section": (s + i) % S}, device_id_type=MESH)
    pl.semaphore_wait(barrier, R + S)

    def exchange(j):
        return pltpu.make_async_remote_copy(
            src_ref=packed.at[peer(j)], dst_ref=pbuf.at[0, j], send_sem=a_send.at[j], recv_sem=p_recv.at[0, j],
            device_id={"row": peer(j)}, device_id_type=MESH)

    def gather(j):
        return pltpu.make_async_remote_copy(
            src_ref=coeffs, dst_ref=qbuf.at[j], send_sem=q_send.at[j], recv_sem=q_recv.at[j],
            device_id={"row": peer(j)}, device_id_type=MESH)

    def forward(t, j):
        return pltpu.make_async_remote_copy(
            src_ref=pbuf.at[t, j], dst_ref=pbuf.at[t + 1, j], send_sem=p_send.at[t, j], recv_sem=p_recv.at[t + 1, j],
            device_id={"col": right}, device_id_type=MESH)

    own_p = pltpu.make_async_copy(packed.at[r], pbuf.at[0, 0], loc_sem.at[0])
    own_q = pltpu.make_async_copy(coeffs, qbuf.at[0], loc_sem.at[1])
    own_p.start()
    for j in range(1, R):
        exchange(j).start()
    own_p.wait()
    forward(0, 0).start()
    own_q.start()
    for j in range(1, R):
        gather(j).start()
    for j in range(1, R):
        exchange(j).wait_recv()
        forward(0, j).start()
    for t in range(1, C - 1):
        for j in range(R):
            forward(t - 1, j).wait_recv()
            forward(t, j).start()

    def product(t, j):
        def body(n, carry):
            at = pl.ds(pl.multiple_of(n * step, step), step)
            term = jnp.dot(pbuf[t, j], qbuf[j, :, at], preferred_element_type=jnp.float32)
            if j == 0:
                tiles[t, :, at] = term
            else:
                tiles[t, :, at] += term
            return carry

        lax.fori_loop(0, columns // step, body, 0)

    def to_owner(t):
        origin = (z + C - t) % C
        owner, place = origin // shares, origin % shares
        return owner, pltpu.make_async_remote_copy(
            src_ref=tiles.at[t], dst_ref=parts.at[place, (s + S - owner) % S], send_sem=f_send.at[t],
            recv_sem=f_recv.at[place, (s + S - owner) % S], device_id={"section": owner}, device_id_type=MESH)

    def to_row(t):
        origin = (z + C - t) % C
        place = origin % shares
        return place, pltpu.make_async_remote_copy(
            src_ref=tiles.at[t], dst_ref=out.at[share], send_sem=y_send.at[t], recv_sem=y_recv.at[share],
            device_id={"row": place * blocks + half}, device_id_type=MESH)

    def hand_over(t):
        owner, copy = to_owner(t)

        @pl.when(s != owner)
        def _():
            copy.start()

    def settle(t):
        owner, _unused = to_owner(t)
        place, copy = to_row(t)

        @pl.when(s == owner)
        def _():
            for i in range(1, S):
                pltpu.make_async_copy(parts.at[place, i], parts.at[place, i], f_recv.at[place, i]).wait()

            def body(n, carry):
                rows = pl.ds(pl.multiple_of(n * 16, 16), 16)
                total = tiles[t, rows, :]
                for i in range(1, S):
                    total = total + parts[place, i, rows, :]
                tiles[t, rows, :] = total
                return carry

            lax.fori_loop(0, width // 16, body, 0)

            @pl.when(place == share)
            def _():
                keep = pltpu.make_async_copy(tiles.at[t], out.at[share], loc_sem.at[2])
                keep.start()
                keep.wait()

            @pl.when(place != share)
            def _():
                copy.start()

    own_q.wait()
    for j in range(R):
        if j > 0:
            gather(j).wait_recv()

        def each(t, carry, j=j):
            product(t, j)
            return carry

        lax.fori_loop(0, C - 1, each, 0)
    for t in range(C - 1):
        hand_over(t)
    for t in range(C - 1):
        settle(t)
    for j in range(R):
        forward(C - 2, j).wait_recv()
        product(C - 1, j)
    hand_over(C - 1)
    settle(C - 1)

    for j in range(1, R):
        exchange(j).wait_send()
        gather(j).wait_send()
    for t in range(C - 1):
        for j in range(R):
            forward(t, j).wait_send()
    for t in range(C):
        owner, copy = to_owner(t)
        place, row_copy = to_row(t)

        @pl.when(s != owner)
        def _(copy=copy):
            copy.wait_send()

        @pl.when((s == owner) & (place != share))
        def _(row_copy=row_copy):
            row_copy.wait_send()

    for e in range(shares):

        @pl.when(share != e)
        def _(e=e):
            pltpu.make_async_copy(out.at[e], out.at[e], y_recv.at[e]).wait()


def per_device(sizes, coeffs, occ_energy, vir_energy, frequency):
    S, R, C = sizes
    energy_gap = vir_energy[None, :] - occ_energy[:, None]
    factor = 2.0 * energy_gap / (energy_gap * energy_gap + frequency * frequency)
    scaled = (coeffs.astype(jnp.float32) * factor[:, :, None]).astype(jnp.bfloat16)
    occupied, local_vir, columns = coeffs.shape
    depth = occupied * local_vir
    blocks = S * R // C
    shares = R // blocks
    width = columns // R
    packed = scaled.reshape(depth, blocks, shares, width).transpose(2, 1, 3, 0).reshape(R, width, depth)
    sem = pltpu.SemaphoreType.DMA
    out = pl.pallas_call(
        functools.partial(response_kernel, S, R, C),
        out_shape=jax.ShapeDtypeStruct((shares, width, columns), jnp.float32),
        in_specs=[pl.BlockSpec(memory_space=pl.ANY)] * 2,
        out_specs=pl.BlockSpec(memory_space=pltpu.VMEM),
        scratch_shapes=[
            pltpu.VMEM((C, R, width, depth), jnp.bfloat16),
            pltpu.VMEM((R, depth, columns), jnp.bfloat16),
            pltpu.VMEM((C, width, columns), jnp.float32),
            pltpu.VMEM((shares, S, width, columns), jnp.float32),
            sem((3,)), sem((C, R)), sem((C, R)), sem((R,)), sem((R,)), sem((R,)),
            sem((C,)), sem((shares, S)), sem((C,)), sem((shares,)),
        ],
        compiler_params=pltpu.CompilerParams(collective_id=0, has_side_effects=True, vmem_limit_bytes=60 * 1024 * 1024),
        cost_estimate=pl.CostEstimate(flops=2 * C * R * width * depth * columns, bytes_accessed=8 * depth * columns, transcendentals=0),
    )(packed, coeffs.reshape(depth, columns))
    return out.reshape(shares * width, columns)


def solution(mesh):
    placed = (P("section", "row", "col"), P("section"), P("row"), P())
    sizes = (mesh.shape["section"], mesh.shape["row"], mesh.shape["col"])
    return jax.shard_map(
        functools.partial(per_device, sizes),
        mesh=mesh,
        in_specs=placed,
        out_specs=P(("section", "row"), "col"),
        check_vma=False,
    )
```

```python
import functools

import jax
import jax.numpy as jnp
from jax import lax
from jax.experimental import pallas as pl
from jax.experimental.pallas import tpu as pltpu
from jax.sharding import PartitionSpec as P

MESH = pl.DeviceIdType.MESH


PIECES = 3


def response_kernel(S, R, C, N, factor, coeffs, out, packed, pbuf, qbuf, tiles, parts, loc_sem, p_send, p_recv, a_send, q_send, q_recv, f_send, f_recv, y_send, y_recv):
    width, depth = packed.shape[1], packed.shape[2]
    columns = coeffs.shape[1]
    blocks = S * R // C
    shares = R // blocks
    piece = width // N
    step = columns // 3 if columns % 384 == 0 else columns
    s = lax.axis_index("section")
    r = lax.axis_index("row")
    z = lax.axis_index("col")
    share, half = r // blocks, r % blocks
    right, left = (z + 1) % C, (z + C - 1) % C

    def peer(j):
        total, unit = 0, 1
        while unit < R:
            total = total + ((r // unit + j // unit) % 2) * unit
            unit *= 2
        return total

    def rows(c):
        return pl.ds(pl.multiple_of(c * piece, piece), piece)

    own_q = pltpu.make_async_copy(coeffs, qbuf.at[0], loc_sem.at[0])
    own_q.start()
    barrier = pltpu.get_barrier_semaphore()
    for j in range(1, R):
        pl.semaphore_signal(barrier, inc=1, device_id={"row": peer(j)}, device_id_type=MESH)
    for other in (left, right):
        pl.semaphore_signal(barrier, inc=1, device_id={"col": other}, device_id_type=MESH)
    for i in range(1, S):
        pl.semaphore_signal(barrier, inc=1, device_id={"section": (s + i) % S}, device_id_type=MESH)

    def exchange(j, c):
        return pltpu.make_async_remote_copy(
            src_ref=packed.at[peer(j), rows(c)], dst_ref=pbuf.at[0, j, rows(c)], send_sem=a_send.at[j, c],
            recv_sem=p_recv.at[0, j, c], device_id={"row": peer(j)}, device_id_type=MESH)

    def gather(j):
        return pltpu.make_async_remote_copy(
            src_ref=coeffs, dst_ref=qbuf.at[j], send_sem=q_send.at[j], recv_sem=q_recv.at[j],
            device_id={"row": peer(j)}, device_id_type=MESH)

    def forward(t, j, c):
        return pltpu.make_async_remote_copy(
            src_ref=pbuf.at[t, j, rows(c)], dst_ref=pbuf.at[t + 1, j, rows(c)], send_sem=p_send.at[t, j, c],
            recv_sem=p_recv.at[t + 1, j, c], device_id={"col": right}, device_id_type=MESH)

    def loop(count, body):
        def run(n, carry):
            body(n)
            return carry

        lax.fori_loop(0, count, run, 0)

    own_q.wait()
    chunk = min(256, depth)
    for d in range(R):
        first = ((d % blocks) * shares + d // blocks) * width

        def pack(n, d=d, first=first):
            at = pl.ds(pl.multiple_of(n * chunk, chunk), chunk)
            value = qbuf[0, at, first:first + width].astype(jnp.float32) * factor[at, :]
            packed[d, :, at] = value.astype(jnp.bfloat16).T

        loop(depth // chunk, pack)
    own_p = pltpu.make_async_copy(packed.at[r], pbuf.at[0, 0], loc_sem.at[1])
    own_p.start()
    pl.semaphore_wait(barrier, R + S)

    def spread(c):
        for j in range(1, R):
            exchange(j, c).start()

    loop(N, spread)
    own_p.wait()
    forward(0, 0, 0).start()
    for j in range(1, R):
        gather(j).start()

    def begin(c):
        for j in range(1, R):
            exchange(j, c).wait_recv()
            forward(0, j, c).start()

    begin(0)

    def begin_next(c):
        forward(0, 0, c + 1).start()
        begin(c + 1)

    loop(N - 1, begin_next)
    for t in range(1, C - 1):

        def relay(c, t=t):
            for j in range(R):
                forward(t - 1, j, c).wait_recv()
                forward(t, j, c).start()

        loop(N, relay)

    def product(t, at_rows, j):
        def body(n):
            at = pl.ds(pl.multiple_of(n * step, step), step)
            term = jnp.dot(pbuf[t, j, at_rows, :], qbuf[j, :, at], preferred_element_type=jnp.float32)
            if j == 0:
                tiles[t, at_rows, at] = term
            else:
                tiles[t, at_rows, at] += term

        loop(columns // step, body)

    def target(t):
        origin = (z + C - t) % C
        return origin // shares, origin % shares

    def to_owner(t, c):
        owner, place = target(t)
        return pltpu.make_async_remote_copy(
            src_ref=tiles.at[t, rows(c)], dst_ref=parts.at[place, (s + S - owner) % S, rows(c)],
            send_sem=f_send.at[t, c], recv_sem=f_recv.at[place, (s + S - owner) % S, c],
            device_id={"section": owner}, device_id_type=MESH)

    def to_row(t, c):
        place = target(t)[1]
        return pltpu.make_async_remote_copy(
            src_ref=tiles.at[t, rows(c)], dst_ref=out.at[share, rows(c)], send_sem=y_send.at[t, c],
            recv_sem=y_recv.at[share, c], device_id={"row": place * blocks + half}, device_id_type=MESH)

    def hand_over(t, c):
        @pl.when(s != target(t)[0])
        def _():
            to_owner(t, c).start()

    def settle(t, c):
        owner, place = target(t)

        @pl.when(s == owner)
        def _():
            for i in range(1, S):
                arrived = parts.at[place, i, rows(c)]
                pltpu.make_async_copy(arrived, arrived, f_recv.at[place, i, c]).wait()

            def add(n):
                at = pl.ds(pl.multiple_of(c * piece + n * 16, 16), 16)
                total = tiles[t, at, :]
                for i in range(1, S):
                    total = total + parts[place, i, at, :]
                tiles[t, at, :] = total

            loop(piece // 16, add)

            @pl.when(place == share)
            def _():
                keep = pltpu.make_async_copy(tiles.at[t, rows(c)], out.at[share, rows(c)], loc_sem.at[2])
                keep.start()
                keep.wait()

            @pl.when(place != share)
            def _():
                to_row(t, c).start()

    for j in range(R):
        if j > 0:
            gather(j).wait_recv()
        loop(C - 1, lambda t, j=j: product(t, pl.ds(0, width), j))
    loop((C - 1) * N, lambda n: hand_over(n // N, n % N))
    loop((C - 1) * N, lambda n: settle(n // N, n % N))

    def finish(c):
        for j in range(R):
            forward(C - 2, j, c).wait_recv()
            product(C - 1, rows(c), j)
        hand_over(C - 1, c)
        settle(C - 1, c)

    loop(N, finish)

    def drain(c):
        for j in range(1, R):
            exchange(j, c).wait_send()
        for t in range(C - 1):
            for j in range(R):
                forward(t, j, c).wait_send()
        for e in range(shares):

            @pl.when(share != e)
            def _(e=e):
                pltpu.make_async_copy(out.at[e, rows(c)], out.at[e, rows(c)], y_recv.at[e, c]).wait()

    def drain_tiles(n):
        t, c = n // N, n % N
        owner, place = target(t)

        @pl.when(s != owner)
        def _():
            to_owner(t, c).wait_send()

        @pl.when((s == owner) & (place != share))
        def _():
            to_row(t, c).wait_send()

    for j in range(1, R):
        gather(j).wait_send()
    loop(C * N, drain_tiles)
    loop(N, drain)


def per_device(sizes, coeffs, occ_energy, vir_energy, frequency):
    S, R, C = sizes
    energy_gap = vir_energy[None, :] - occ_energy[:, None]
    factor = 2.0 * energy_gap / (energy_gap * energy_gap + frequency * frequency)
    occupied, local_vir, columns = coeffs.shape
    depth = occupied * local_vir
    blocks = S * R // C
    shares = R // blocks
    width = columns // R
    N = PIECES if width % (16 * PIECES) == 0 else 1
    sem = pltpu.SemaphoreType.DMA
    out = pl.pallas_call(
        functools.partial(response_kernel, S, R, C, N),
        out_shape=jax.ShapeDtypeStruct((shares, width, columns), jnp.float32),
        in_specs=[pl.BlockSpec(memory_space=pltpu.VMEM), pl.BlockSpec(memory_space=pl.ANY)],
        out_specs=pl.BlockSpec(memory_space=pltpu.VMEM),
        scratch_shapes=[
            pltpu.VMEM((R, width, depth), jnp.bfloat16),
            pltpu.VMEM((C, R, width, depth), jnp.bfloat16),
            pltpu.VMEM((R, depth, columns), jnp.bfloat16),
            pltpu.VMEM((C, width, columns), jnp.float32),
            pltpu.VMEM((shares, S, width, columns), jnp.float32),
            sem((3,)), sem((C, R, N)), sem((C, R, N)), sem((R, N)), sem((R,)), sem((R,)),
            sem((C, N)), sem((shares, S, N)), sem((C, N)), sem((shares, N)),
        ],
        compiler_params=pltpu.CompilerParams(collective_id=0, has_side_effects=True, vmem_limit_bytes=60 * 1024 * 1024),
        cost_estimate=pl.CostEstimate(flops=2 * C * R * width * depth * columns, bytes_accessed=8 * depth * columns, transcendentals=0),
    )(factor.reshape(depth, 1), coeffs.reshape(depth, columns))
    return out.reshape(shares * width, columns)


def solution(mesh):
    placed = (P("section", "row", "col"), P("section"), P("row"), P())
    sizes = (mesh.shape["section"], mesh.shape["row"], mesh.shape["col"])
    return jax.shard_map(
        functools.partial(per_device, sizes),
        mesh=mesh,
        in_specs=placed,
        out_specs=P(("section", "row"), "col"),
        check_vma=False,
    )
```

```python
import functools

import jax
import jax.numpy as jnp
from jax import lax
from jax.experimental import pallas as pl
from jax.experimental.pallas import tpu as pltpu
from jax.sharding import PartitionSpec as P

MESH = pl.DeviceIdType.MESH


PIECES = 3


def response_kernel(S, R, C, N, factor, coeffs, out, raw, scale, fbuf, qbuf, pbuf, lbuf, tiles, parts, edge, edge_parts, edge_in, inbox,
                    loc_sem, fac_send, fac_recv, q_send, q_recv, p_send, p_recv, f_send, f_recv, y_send, y_recv,
                    e_send, e_recv, ez_send, ez_recv, ey_send, ey_recv):
    depth, columns = coeffs.shape
    width = columns // R
    blocks = S * R // C
    shares = R // blocks
    tall = shares * width
    piece = width // N
    lean = C >= 4
    step = columns // 3 if columns % 384 == 0 else columns
    s = lax.axis_index("section")
    r = lax.axis_index("row")
    z = lax.axis_index("col")
    share, half = r // blocks, r % blocks
    is_end = (z == 0) | (z == C - 1) if lean else z < 0
    is_near = (z == 1) | (z == C - 2) if lean else z < 0
    is_last = (z == 0) | (z == C - 1) if C > 2 else z < 0
    near = jnp.where(z == 0, 1, C - 2)
    end = jnp.where(z == 1, 0, C - 1)

    def peer(j):
        total, unit = 0, 1
        while unit < R:
            total = total + ((r // unit + j // unit) % 2) * unit
            unit *= 2
        return total

    def strip(row):
        first = ((row % blocks) * shares + row // blocks) * width
        return pl.ds(first if isinstance(row, int) else pl.multiple_of(first, width), width)

    def rows(c):
        return pl.ds(pl.multiple_of(c * piece, piece), piece)

    def loop(count, body):
        def run(n, carry):
            body(n)
            return carry

        lax.fori_loop(0, count, run, 0)

    def remote(source, there, sent, landed, **device):
        return pltpu.make_async_remote_copy(
            src_ref=source, dst_ref=there, send_sem=sent, recv_sem=landed, device_id=device, device_id_type=MESH)

    own = pltpu.make_async_copy(coeffs, raw, loc_sem.at[0])
    own.start()
    barrier = pltpu.get_barrier_semaphore()
    for j in range(1, R):
        pl.semaphore_signal(barrier, inc=1, device_id={"row": peer(j)}, device_id_type=MESH)
    for other in ((z + C - 1) % C, (z + 1) % C):
        pl.semaphore_signal(barrier, inc=1, device_id={"col": other}, device_id_type=MESH)
    for i in range(1, S):
        pl.semaphore_signal(barrier, inc=1, device_id={"section": (s + i) % S}, device_id_type=MESH)
    own.wait()
    chunk = min(256, depth)

    def turn(n):
        at = pl.ds(pl.multiple_of(n * chunk, chunk), chunk)
        qbuf[0, :, at] = raw[at, :].T

    loop(depth // chunk, turn)
    fbuf[0] = factor[...]
    pl.semaphore_wait(barrier, R + S)

    def give_factor(j):
        return remote(factor, fbuf.at[j], fac_send.at[j], fac_recv.at[j], row=peer(j))

    def gather(source, j, k, via):
        at = strip(peer(k))
        return remote(qbuf.at[source, at], qbuf.at[j, at], q_send.at[j, k], q_recv.at[j, k], row=peer(via))

    def landed(j, k):
        at = strip(peer(j ^ k))
        pltpu.make_async_copy(qbuf.at[j, at], qbuf.at[j, at], q_recv.at[j, k]).wait()

    direct = [j for j in range(1, R) if j & (j - 1) == 0]
    relayed = [j for j in range(1, R) if j & (j - 1)]

    def relay(j, k):
        low = j & -j
        via, kept = (low, j - low) if k % 2 else (j - low, low)
        at = strip(peer(via ^ j ^ k))
        return kept, remote(qbuf.at[kept, at], qbuf.at[j, at], q_send.at[j, k], q_recv.at[j, k], row=peer(via))

    def own_strip(j):
        return qbuf.at[j, strip(r)]

    def send_right(source, t, j, c):
        return remote(source, pbuf.at[t, j, rows(c)], p_send.at[0, t, j, c], p_recv.at[t, j, c], col=jnp.minimum(z + 1, C - 1))

    def send_left(source, t, j, c):
        return remote(source, pbuf.at[t, j, rows(c)], p_send.at[1, t, j, c], p_recv.at[t, j, c], col=jnp.maximum(z - 1, 0))

    own_right = (z < C - 1) & (z != C - 2) if lean else z < C - 1
    own_left = (z > 0) & (z != 1) if lean else z > 0

    def broadcast(j):
        def one(c):
            first = ((r % blocks) * shares + r // blocks) * width
            source = qbuf.at[j, pl.ds(pl.multiple_of(first + c * piece, piece), piece)]

            @pl.when(own_right)
            def _():
                send_right(source, z, j, c).start()

            @pl.when(own_left)
            def _():
                send_left(source, z, j, c).start()

        loop(N, one)

    for j in range(1, R):
        give_factor(j).start()
    def order(j):
        return sorted(range(R), key=lambda k: (k != j, k % 2 != (0 if j % 2 else 1), -k))

    arrived = set()

    def ensure(j, k):
        if (j, k) not in arrived:
            arrived.add((j, k))
            landed(j, k)

    def pass_on(j, k):
        kept, copy = relay(j, k)
        ensure(kept, k)
        copy.start()

    quick = 2 if len(relayed) == 1 else R
    for n in range(quick):
        for j in direct:
            gather(0, j, order(j)[n], j).start()
    broadcast(0)
    for j in direct:
        ensure(j, j)
        broadcast(j)
    for j in relayed:
        for n, k in enumerate(reversed(range(R))):
            if n == quick:
                for late in range(quick, R):
                    for i in direct:
                        gather(0, i, order(i)[late], i).start()
                ensure(j, j)
                broadcast(j)
            pass_on(j, k)
        if quick == R:
            ensure(j, j)
            broadcast(j)

    def take(t, j, c):
        pltpu.make_async_copy(pbuf.at[t, j, rows(c)], pbuf.at[t, j, rows(c)], p_recv.at[t, j, c]).wait()

    def from_left(i):
        return (z >= i) & jnp.logical_not(is_end & (z == C - 1) & (i == 1)) if lean else z >= i

    def from_right(i):
        return (z + i < C) & jnp.logical_not(is_end & (z == 0) & (i == 1)) if lean else z + i < C

    def visit(i, j, c, wait, onward_right, onward_left):
        @pl.when(from_left(i))
        def _():
            if wait:
                take(z - i, j, c)

            @pl.when(onward_right)
            def _():
                send_right(pbuf.at[z - i, j, rows(c)], z - i, j, c).start()

        @pl.when(from_right(i))
        def _():
            if wait:
                take(z + i, j, c)

            @pl.when(onward_left)
            def _():
                send_left(pbuf.at[z + i, j, rows(c)], z + i, j, c).start()

    go_right, go_left = z < C - 1, z > 0
    for j in range(R):
        loop(N, lambda c, j=j: visit(1, j, c, True, go_right & jnp.logical_not(own_right), go_left & jnp.logical_not(own_left)))

    def second(c):
        for j in range(R):
            visit(1, j, c, False, go_right & own_right, go_left & own_left)

    loop(N, second)

    def times(value, j):
        return (value.astype(jnp.float32) * fbuf[j, 0:1, :]).astype(jnp.bfloat16)

    def dot(x, y):
        return lax.dot_general(x, y, (((1,), (1,)), ((), ())), preferred_element_type=jnp.float32)

    def product(t, load, at_rows, j):
        lbuf[at_rows, :] = times(load(), j)

        def body(n):
            at = pl.ds(pl.multiple_of(n * step, step), step)
            term = dot(lbuf[at_rows, :], qbuf[j, at, :])
            if j == 0:
                tiles[t, at_rows, at] = term
            else:
                tiles[t, at_rows, at] += term

        loop(columns // step, body)

    def target(t):
        return t // shares, t % shares

    def to_owner(t, c):
        owner, place = target(t)
        index = (s + S - owner + S - 1) % S
        return remote(tiles.at[t, rows(c)], parts.at[place, index, rows(c)], f_send.at[t, c], f_recv.at[place, index, c], section=owner)

    def to_row(t, c):
        return remote(tiles.at[t, rows(c)], out.at[share, rows(c)], y_send.at[t, c], y_recv.at[share, c], row=target(t)[1] * blocks + half)

    def hand_over(t, c):
        @pl.when(s != target(t)[0])
        def _():
            to_owner(t, c).start()

    def settle(t, c):
        owner, place = target(t)

        @pl.when(s == owner)
        def _():
            for i in range(S - 1):
                came = parts.at[place, i, rows(c)]
                pltpu.make_async_copy(came, came, f_recv.at[place, i, c]).wait()

            def add(n):
                at = pl.ds(pl.multiple_of(c * piece + n * 16, 16), 16)
                total = tiles[t, at, :]
                for i in range(S - 1):
                    total = total + parts[place, i, at, :]
                tiles[t, at, :] = total

            loop(piece // 16, add)

            @pl.when(place == share)
            def _():
                keep = pltpu.make_async_copy(tiles.at[t, rows(c)], out.at[share, rows(c)], loc_sem.at[1])
                keep.start()
                keep.wait()

            @pl.when(place != share)
            def _():
                to_row(t, c).start()

    edge_owner, edge_place = target(z)
    near_owner, near_place = target(near)

    def edge_rows(h):
        return pl.ds(pl.multiple_of(h * tall, tall), tall)

    def edge_to_owner(h):
        index = (s + S - edge_owner + S - 1) % S
        return remote(edge.at[edge_rows(h)], edge_parts.at[index, edge_rows(h)], e_send.at[h], e_recv.at[index, h], section=edge_owner)

    def edge_out(h):
        return remote(edge.at[edge_rows(h)], edge_in.at[edge_rows(h)], ez_send.at[h], ez_recv.at[h], col=end)

    def edge_to_row(h):
        return remote(edge_in.at[edge_rows(h)], inbox.at[r], ey_send.at[h], ey_recv.at[r], row=near_place * blocks + h)

    def edge_unit(j):
        def body(n):
            at = pl.ds(pl.multiple_of(n * step, step), step)
            term = dot(times(qbuf[j, at, :], j), pbuf[end, j])
            if j == 0:
                edge[at, :] = term
            else:
                edge[at, :] += term

        loop(columns // step, body)

    def edge_hand():
        @pl.when(s != edge_owner)
        def _():
            for h in range(blocks):
                edge_to_owner(h).start()

    def edge_settle():
        @pl.when(s == edge_owner)
        def _():
            for h in range(blocks):
                for i in range(S - 1):
                    came = edge_parts.at[i, edge_rows(h)]
                    pltpu.make_async_copy(came, came, e_recv.at[i, h]).wait()

                def add(n, h=h):
                    at = pl.ds(pl.multiple_of(h * tall + n * 16, 16), 16)
                    total = edge[at, :]
                    for i in range(S - 1):
                        total = total + edge_parts[i, at, :]
                    edge[at, :] = total

                loop(tall // 16, add)
                edge_out(h).start()

    def edge_pass():
        for h in range(blocks):
            came = edge_in.at[edge_rows(h)]
            pltpu.make_async_copy(came, came, ez_recv.at[h]).wait()
            goal = near_place * blocks + h

            @pl.when(goal != r)
            def _(h=h):
                edge_to_row(h).start()

            @pl.when(goal == r)
            def _(h=h):
                keep = pltpu.make_async_copy(edge_in.at[edge_rows(h)], inbox.at[r], loc_sem.at[2])
                keep.start()
                keep.wait()

    takes_edge = is_end & (s == near_owner) & (share == near_place)

    def edge_place_all():
        for row in range(R):
            @pl.when(r != row)
            def _(row=row):
                pltpu.make_async_copy(inbox.at[row], inbox.at[row], ey_recv.at[row]).wait()

        first = [((row % blocks) * shares + row // blocks) * width for row in range(R)]
        for row in range(R):
            for e in range(shares):
                def put(n, row=row, e=e):
                    at = pl.ds(pl.multiple_of(n * 16, 16), 16)
                    out[e, at, first[row]:first[row] + width] = inbox[row, pl.ds(pl.multiple_of(e * width + n * 16, 16), 16), :]

                loop(width // 16, put)

    def rest(j):
        for k in range(R):
            if j:
                ensure(j, k)
        if j:
            give_factor(j).wait_recv()

    def pieces(t, c):
        for j in range(R):
            product(t, lambda j=j: pbuf[t, j, rows(c), :], rows(c), j)
        hand_over(t, c)
        settle(t, c)

    every = pl.ds(0, width)

    def own_unit(j):
        product(z, lambda: qbuf[j, strip(r), :], every, j)

    def left_unit(j):
        pl.when(from_left(1))(lambda: product(z - 1, lambda: pbuf[z - 1, j], every, j))

    def right_unit(j):
        pl.when(from_right(1))(lambda: product(z + 1, lambda: pbuf[z + 1, j], every, j))

    def near_unit(j):
        if lean:
            pl.when(is_near)(lambda: edge_unit(j))

    def near_step(work):
        if lean:
            pl.when(is_near)(work)

    def whole_slot(action):
        action(z)
        pl.when(from_left(1))(lambda: action(z - 1))
        pl.when(from_right(1))(lambda: action(z + 1))

    def hand_all(t):
        loop(N, lambda c: hand_over(t, c))

    def settle_all(t):
        loop(N, lambda c: settle(t, c))

    units = [(0, own_unit, 0), (1, near_unit, 0), (2, left_unit, 0), (3, right_unit, 0)]
    units += [(6 if j < R - 1 else 7, near_unit, j) for j in range(1, R)]
    units += [(7, lambda j: near_step(edge_hand), 0), (8, lambda j: near_step(edge_settle), 0)]
    units += [(8 if j == 1 else 9, own_unit, j) for j in range(1, R)]
    units += [(10 if j < R - 1 else 11, left_unit, j) for j in range(1, R)]
    units += [(11, right_unit, j) for j in range(1, R)]
    visits = N * R if C > 3 else 0
    ready = {0}

    def run(unit):
        when, work, j = unit
        if j not in ready:
            ready.add(j)
            rest(j)
        work(j)

    queue = list(units)
    for v in range(visits):
        visit(2, v % R, v // R, True, go_right, go_left)
        while queue and queue[0][0] * visits <= v * 12:
            run(queue.pop(0))
    for unit in queue:
        run(unit)
    for j in range(R):
        if j not in ready:
            rest(j)
    for i in range(3, C - 1):
        def onward(c, i=i):
            for j in range(R):
                visit(i, j, c, True, go_right, go_left)

        loop(N, onward)
    whole_slot(hand_all)
    whole_slot(settle_all)
    for i in range(2, C - 1):
        @pl.when(from_left(i))
        def _(i=i):
            loop(N, lambda c: pieces(z - i, c))

        @pl.when(from_right(i))
        def _(i=i):
            loop(N, lambda c: pieces(z + i, c))

    @pl.when(is_last)
    def _():
        other = C - 1 - z

        def finish(c):
            for j in range(R):
                take(other, j, c)
            pieces(other, c)

        loop(N, finish)

    if lean:
        pl.when(is_end & (s == near_owner))(edge_pass)
        pl.when(takes_edge)(edge_place_all)

    for j in range(1, R):
        give_factor(j).wait_send()
    for j in direct:
        for k in range(R):
            gather(0, j, k, j).wait_send()
    for j in relayed:
        for k in range(R):
            relay(j, k)[1].wait_send()

    def drain(c):
        for j in range(R):
            @pl.when(own_right)
            def _(j=j):
                send_right(pbuf.at[z, j, rows(c)], z, j, c).wait_send()

            @pl.when(own_left)
            def _(j=j):
                send_left(pbuf.at[z, j, rows(c)], z, j, c).wait_send()

            for i in range(1, C - 1):
                @pl.when(from_left(i) & go_right)
                def _(i=i, j=j):
                    send_right(pbuf.at[z - i, j, rows(c)], z - i, j, c).wait_send()

                @pl.when(from_right(i) & go_left)
                def _(i=i, j=j):
                    send_left(pbuf.at[z + i, j, rows(c)], z + i, j, c).wait_send()

        for e in range(shares):
            @pl.when((share != e) & jnp.logical_not(takes_edge))
            def _(e=e):
                pltpu.make_async_copy(out.at[e, rows(c)], out.at[e, rows(c)], y_recv.at[e, c]).wait()

        for t in range(C):
            owner, place = target(t)
            used = jnp.logical_not(is_end & (near == t))

            @pl.when(used & (s != owner))
            def _(t=t):
                to_owner(t, c).wait_send()

            @pl.when(used & (s == owner) & (place != share))
            def _(t=t):
                to_row(t, c).wait_send()

    loop(N, drain)
    if lean:
        for h in range(blocks):
            @pl.when(is_near & (s != edge_owner))
            def _(h=h):
                edge_to_owner(h).wait_send()

            @pl.when(is_near & (s == edge_owner))
            def _(h=h):
                edge_out(h).wait_send()

            @pl.when(is_end & (s == near_owner) & (near_place * blocks + h != r))
            def _(h=h):
                edge_to_row(h).wait_send()


def per_device(sizes, coeffs, occ_energy, vir_energy, frequency):
    S, R, C = sizes
    energy_gap = vir_energy[None, :] - occ_energy[:, None]
    factor = 2.0 * energy_gap / (energy_gap * energy_gap + frequency * frequency)
    occupied, local_vir, columns = coeffs.shape
    depth = occupied * local_vir
    blocks = S * R // C
    shares = R // blocks
    width = columns // R
    N = PIECES if width % (16 * PIECES) == 0 else 1
    sem = pltpu.SemaphoreType.DMA
    half, single = jnp.bfloat16, jnp.float32
    out = pl.pallas_call(
        functools.partial(response_kernel, S, R, C, N),
        out_shape=jax.ShapeDtypeStruct((shares, width, columns), jnp.float32),
        in_specs=[pl.BlockSpec(memory_space=pltpu.VMEM), pl.BlockSpec(memory_space=pl.ANY)],
        out_specs=pl.BlockSpec(memory_space=pltpu.VMEM),
        scratch_shapes=[
            pltpu.VMEM((depth, columns), half),
            pltpu.VMEM((8, depth), single),
            pltpu.VMEM((R, 8, depth), single),
            pltpu.VMEM((R, columns, depth), half),
            pltpu.VMEM((C, R, width, depth), half),
            pltpu.VMEM((width, depth), half),
            pltpu.VMEM((C, width, columns), single),
            pltpu.VMEM((shares, S - 1, width, columns), single),
            pltpu.VMEM((columns, width), single),
            pltpu.VMEM((S - 1, columns, width), single),
            pltpu.VMEM((columns, width), single),
            pltpu.VMEM((R, shares * width, width), single),
            sem((3,)), sem((R,)), sem((R,)), sem((R, R)), sem((R, R)), sem((2, C, R, N)), sem((C, R, N)),
            sem((C, N)), sem((shares, S - 1, N)), sem((C, N)), sem((shares, N)),
            sem((blocks,)), sem((S - 1, blocks)), sem((blocks,)), sem((blocks,)), sem((blocks,)), sem((R,)),
        ],
        compiler_params=pltpu.CompilerParams(collective_id=0, has_side_effects=True, vmem_limit_bytes=62 * 1024 * 1024),
        cost_estimate=pl.CostEstimate(flops=2 * C * R * width * depth * columns, bytes_accessed=8 * depth * columns, transcendentals=0),
    )(jnp.broadcast_to(factor.reshape(1, depth), (8, depth)), coeffs.reshape(depth, columns))
    return out.reshape(shares * width, columns)


def solution(mesh):
    placed = (P("section", "row", "col"), P("section"), P("row"), P())
    sizes = (mesh.shape["section"], mesh.shape["row"], mesh.shape["col"])
    return jax.shard_map(
        functools.partial(per_device, sizes),
        mesh=mesh,
        in_specs=placed,
        out_specs=P(("section", "row"), "col"),
        check_vma=False,
    )
```

```python
import functools

import jax
import jax.numpy as jnp
from jax import lax
from jax.experimental import pallas as pl
from jax.experimental.pallas import tpu as pltpu
from jax.sharding import PartitionSpec as P

MESH = pl.DeviceIdType.MESH


PIECES = 3


def response_kernel(S, R, C, N, factor, coeffs, out, raw, scale, fbuf, qbuf, pbuf, lbuf, tiles, parts, edge, edge_parts, edge_in, inbox,
                    loc_sem, fac_send, fac_recv, q_send, q_recv, p_send, p_recv, f_send, f_recv, y_send, y_recv,
                    e_send, e_recv, ez_send, ez_recv, ey_send, ey_recv):
    depth, columns = coeffs.shape
    width = columns // R
    blocks = S * R // C
    shares = R // blocks
    tall = shares * width
    piece = width // N
    lean = C >= 4
    step = columns // 3 if columns % 384 == 0 else columns
    s = lax.axis_index("section")
    r = lax.axis_index("row")
    z = lax.axis_index("col")
    share, half = r // blocks, r % blocks
    is_end = (z == 0) | (z == C - 1) if lean else z < 0
    is_near = (z == 1) | (z == C - 2) if lean else z < 0
    is_last = (z == 0) | (z == C - 1) if C > 2 else z < 0
    near = jnp.where(z == 0, 1, C - 2)
    end = jnp.where(z == 1, 0, C - 1)

    def peer(j):
        total, unit = 0, 1
        while unit < R:
            total = total + ((r // unit + j // unit) % 2) * unit
            unit *= 2
        return total

    def strip(row):
        first = ((row % blocks) * shares + row // blocks) * width
        return pl.ds(first if isinstance(row, int) else pl.multiple_of(first, width), width)

    def rows(c):
        return pl.ds(pl.multiple_of(c * piece, piece), piece)

    def loop(count, body):
        def run(n, carry):
            body(n)
            return carry

        lax.fori_loop(0, count, run, 0)

    def remote(source, there, sent, landed, **device):
        return pltpu.make_async_remote_copy(
            src_ref=source, dst_ref=there, send_sem=sent, recv_sem=landed, device_id=device, device_id_type=MESH)

    own = pltpu.make_async_copy(coeffs, raw, loc_sem.at[0])
    own.start()
    barrier = pltpu.get_barrier_semaphore()
    for j in range(1, R):
        pl.semaphore_signal(barrier, inc=1, device_id={"row": peer(j)}, device_id_type=MESH)
    for other in ((z + C - 1) % C, (z + 1) % C):
        pl.semaphore_signal(barrier, inc=1, device_id={"col": other}, device_id_type=MESH)
    for i in range(1, S):
        pl.semaphore_signal(barrier, inc=1, device_id={"section": (s + i) % S}, device_id_type=MESH)
    own.wait()
    chunk = min(256, depth)

    def turn(n):
        at = pl.ds(pl.multiple_of(n * chunk, chunk), chunk)
        qbuf[0, :, at] = raw[at, :].T

    loop(depth // chunk, turn)
    fbuf[0] = factor[...]
    pl.semaphore_wait(barrier, R + S)

    def give_factor(j):
        return remote(factor, fbuf.at[j], fac_send.at[j], fac_recv.at[j], row=peer(j))

    def gather(source, j, k, via):
        at = strip(peer(k))
        return remote(qbuf.at[source, at], qbuf.at[j, at], q_send.at[j, k], q_recv.at[j, k], row=peer(via))

    def landed(j, k):
        at = strip(peer(j ^ k))
        pltpu.make_async_copy(qbuf.at[j, at], qbuf.at[j, at], q_recv.at[j, k]).wait()

    direct = [j for j in range(1, R) if j & (j - 1) == 0]
    relayed = [j for j in range(1, R) if j & (j - 1)]

    def relay(j, k):
        low = j & -j
        via, kept = (low, j - low) if k % 2 else (j - low, low)
        at = strip(peer(via ^ j ^ k))
        return kept, remote(qbuf.at[kept, at], qbuf.at[j, at], q_send.at[j, k], q_recv.at[j, k], row=peer(via))

    def own_strip(j):
        return qbuf.at[j, strip(r)]

    def send_right(source, t, j, c):
        return remote(source, pbuf.at[t, j, rows(c)], p_send.at[0, t, j, c], p_recv.at[t, j, c], col=jnp.minimum(z + 1, C - 1))

    def send_left(source, t, j, c):
        return remote(source, pbuf.at[t, j, rows(c)], p_send.at[1, t, j, c], p_recv.at[t, j, c], col=jnp.maximum(z - 1, 0))

    own_right = (z < C - 1) & (z != C - 2) if lean else z < C - 1
    own_left = (z > 0) & (z != 1) if lean else z > 0

    def broadcast(j):
        def one(c):
            first = ((r % blocks) * shares + r // blocks) * width
            source = qbuf.at[j, pl.ds(pl.multiple_of(first + c * piece, piece), piece)]

            @pl.when(own_right)
            def _():
                send_right(source, z, j, c).start()

            @pl.when(own_left)
            def _():
                send_left(source, z, j, c).start()

        loop(N, one)

    for j in range(1, R):
        give_factor(j).start()
    arrived = set()

    def ensure(j, k):
        if (j, k) not in arrived:
            arrived.add((j, k))
            landed(j, k)

    by_way = [(j, k) for j in relayed for k in range(1, R) if k != j] if R == 4 else []
    straight = [(j, k) for j in range(1, R) for k in range(R) if (j, k) not in by_way]
    needed = [(relay(j, k)[0], k) for j, k in by_way]
    first = [(j, j) for j in direct]
    second_wave = [(j, j) for j in relayed]
    third = [pair for pair in needed if pair not in first]
    rest_wave = [pair for pair in straight if pair not in first + second_wave + third]

    def issue(pairs):
        for j, k in pairs:
            gather(0, j, k, j).start()

    issue(first)
    broadcast(0)
    for j in direct:
        ensure(j, j)
        if j == 1:
            issue(second_wave)
        broadcast(j)
    issue(third)
    for j in relayed:
        ensure(j, j)
        broadcast(j)
    for (j, k), pair in zip(by_way, needed):
        ensure(*pair)
        relay(j, k)[1].start()
    issue(rest_wave)

    def take(t, j, c):
        pltpu.make_async_copy(pbuf.at[t, j, rows(c)], pbuf.at[t, j, rows(c)], p_recv.at[t, j, c]).wait()

    def from_left(i):
        return (z >= i) & jnp.logical_not(is_end & (z == C - 1) & (i == 1)) if lean else z >= i

    def from_right(i):
        return (z + i < C) & jnp.logical_not(is_end & (z == 0) & (i == 1)) if lean else z + i < C

    def visit(i, j, c, wait, onward_right, onward_left):
        @pl.when(from_left(i))
        def _():
            if wait:
                take(z - i, j, c)

            @pl.when(onward_right)
            def _():
                send_right(pbuf.at[z - i, j, rows(c)], z - i, j, c).start()

        @pl.when(from_right(i))
        def _():
            if wait:
                take(z + i, j, c)

            @pl.when(onward_left)
            def _():
                send_left(pbuf.at[z + i, j, rows(c)], z + i, j, c).start()

    go_right, go_left = z < C - 1, z > 0
    for j in range(R):
        loop(N, lambda c, j=j: visit(1, j, c, True, go_right & jnp.logical_not(own_right), go_left & jnp.logical_not(own_left)))

    def second(c):
        for j in range(R):
            visit(1, j, c, False, go_right & own_right, go_left & own_left)

    loop(N, second)

    def times(value, j):
        return (value.astype(jnp.float32) * fbuf[j, 0:1, :]).astype(jnp.bfloat16)

    def dot(x, y):
        return lax.dot_general(x, y, (((1,), (1,)), ((), ())), preferred_element_type=jnp.float32)

    def product(t, load, at_rows, j):
        lbuf[at_rows, :] = times(load(), j)

        def body(n):
            at = pl.ds(pl.multiple_of(n * step, step), step)
            term = dot(lbuf[at_rows, :], qbuf[j, at, :])
            if j == 0:
                tiles[t, at_rows, at] = term
            else:
                tiles[t, at_rows, at] += term

        loop(columns // step, body)

    def target(t):
        return t // shares, t % shares

    def to_owner(t, c):
        owner, place = target(t)
        index = (s + S - owner + S - 1) % S
        return remote(tiles.at[t, rows(c)], parts.at[place, index, rows(c)], f_send.at[t, c], f_recv.at[place, index, c], section=owner)

    def to_row(t, c):
        return remote(tiles.at[t, rows(c)], out.at[share, rows(c)], y_send.at[t, c], y_recv.at[share, c], row=target(t)[1] * blocks + half)

    def hand_over(t, c):
        @pl.when(s != target(t)[0])
        def _():
            to_owner(t, c).start()

    def settle(t, c):
        owner, place = target(t)

        @pl.when(s == owner)
        def _():
            for i in range(S - 1):
                came = parts.at[place, i, rows(c)]
                pltpu.make_async_copy(came, came, f_recv.at[place, i, c]).wait()

            def add(n):
                at = pl.ds(pl.multiple_of(c * piece + n * 16, 16), 16)
                total = tiles[t, at, :]
                for i in range(S - 1):
                    total = total + parts[place, i, at, :]
                tiles[t, at, :] = total

            loop(piece // 16, add)

            @pl.when(place == share)
            def _():
                keep = pltpu.make_async_copy(tiles.at[t, rows(c)], out.at[share, rows(c)], loc_sem.at[1])
                keep.start()
                keep.wait()

            @pl.when(place != share)
            def _():
                to_row(t, c).start()

    edge_owner, edge_place = target(z)
    near_owner, near_place = target(near)

    strips = blocks * shares

    def edge_rows(h):
        return pl.ds(h % blocks * tall + h // blocks * width, width)

    def edge_to_owner(h):
        index = (s + S - edge_owner + S - 1) % S
        return remote(edge.at[edge_rows(h)], edge_parts.at[index, edge_rows(h)], e_send.at[h], e_recv.at[index, h], section=edge_owner)

    def edge_out(h):
        return remote(edge.at[edge_rows(h)], edge_in.at[edge_rows(h)], ez_send.at[h], ez_recv.at[h], col=end)

    def edge_to_row(h):
        e = h // blocks
        return remote(edge_in.at[edge_rows(h)], inbox.at[r, pl.ds(e * width, width)], ey_send.at[h], ey_recv.at[r, e], row=near_place * blocks + h % blocks)

    def edge_unit(j):
        def body(n):
            at = pl.ds(pl.multiple_of(n * step, step), step)
            term = dot(times(qbuf[j, at, :], j), pbuf[end, j])
            if j == 0:
                edge[at, :] = term
            else:
                edge[at, :] += term

        loop(columns // step, body)

    def edge_hand():
        @pl.when(s != edge_owner)
        def _():
            for h in range(strips):
                edge_to_owner(h).start()

    def edge_settle():
        @pl.when(s == edge_owner)
        def _():
            for h in range(strips):
                for i in range(S - 1):
                    came = edge_parts.at[i, edge_rows(h)]
                    pltpu.make_async_copy(came, came, e_recv.at[i, h]).wait()

                def add(n, h=h):
                    at = pl.ds(pl.multiple_of(h % blocks * tall + h // blocks * width + n * 16, 16), 16)
                    total = edge[at, :]
                    for i in range(S - 1):
                        total = total + edge_parts[i, at, :]
                    edge[at, :] = total

                loop(width // 16, add)
                edge_out(h).start()

    def edge_pass():
        for h in range(strips):
            came = edge_in.at[edge_rows(h)]
            pltpu.make_async_copy(came, came, ez_recv.at[h]).wait()
            goal = near_place * blocks + h % blocks

            @pl.when(goal != r)
            def _(h=h):
                edge_to_row(h).start()

            @pl.when(goal == r)
            def _(h=h):
                there = inbox.at[r, pl.ds(h // blocks * width, width)]
                keep = pltpu.make_async_copy(edge_in.at[edge_rows(h)], there, loc_sem.at[2])
                keep.start()
                keep.wait()

    takes_edge = is_end & (s == near_owner) & (share == near_place)

    def edge_place_all():
        first = [((row % blocks) * shares + row // blocks) * width for row in range(R)]
        for e in range(shares):
            for row in range(R):
                @pl.when(r != row)
                def _(row=row):
                    there = inbox.at[row, pl.ds(e * width, width)]
                    pltpu.make_async_copy(there, there, ey_recv.at[row, e]).wait()

                def put(n, row=row, e=e):
                    at = pl.ds(pl.multiple_of(n * 16, 16), 16)
                    out[e, at, first[row]:first[row] + width] = inbox[row, pl.ds(pl.multiple_of(e * width + n * 16, 16), 16), :]

                loop(width // 16, put)

    def rest(j):
        for k in range(R):
            if j:
                ensure(j, k)
        if j:
            give_factor(j).wait_recv()

    def pieces(t, c):
        for j in range(R):
            product(t, lambda j=j: pbuf[t, j, rows(c), :], rows(c), j)
        hand_over(t, c)
        settle(t, c)

    every = pl.ds(0, width)

    def own_unit(j):
        product(z, lambda: qbuf[j, strip(r), :], every, j)

    def left_unit(j):
        pl.when(from_left(1))(lambda: product(z - 1, lambda: pbuf[z - 1, j], every, j))

    def right_unit(j):
        pl.when(from_right(1))(lambda: product(z + 1, lambda: pbuf[z + 1, j], every, j))

    def near_unit(j):
        if lean:
            pl.when(is_near)(lambda: edge_unit(j))

    def near_step(work):
        if lean:
            pl.when(is_near)(work)

    def hand_all(t):
        loop(N, lambda c: hand_over(t, c))

    def settle_all(t):
        loop(N, lambda c: settle(t, c))

    def on_left(action):
        pl.when(from_left(1))(lambda: action(z - 1))

    def on_right(action):
        pl.when(from_right(1))(lambda: action(z + 1))

    later = 99
    units = [(0, own_unit, 0), (1, near_unit, 0), (2, left_unit, 0), (3, right_unit, 0)]
    units += [(7 + j, near_unit, j) for j in range(1, R)]
    units += [(10, lambda j: near_step(edge_hand), 0)]
    units += [(10 if j == 1 else 11 if j == 2 else later, own_unit, j) for j in range(1, R)]
    units += [(later, lambda j: near_step(edge_settle), 0), (later, lambda j: hand_all(z), 0)]
    units += [(later, left_unit, j) for j in range(1, R)]
    units += [(later, lambda j: on_left(hand_all), 0), (later, lambda j: settle_all(z), 0)]
    units += [(later, right_unit, j) for j in range(1, R)]
    units += [(later, lambda j: on_right(hand_all), 0), (later, lambda j: on_left(settle_all), 0), (later, lambda j: on_right(settle_all), 0)]
    visits = N * R if C > 3 else 0
    ready = {0}

    def run(unit):
        when, work, j = unit
        if j not in ready:
            ready.add(j)
            rest(j)
        work(j)

    queue = list(units)
    for v in range(visits):
        visit(2, v % R, v // R, True, go_right, go_left)
        while queue and queue[0][0] * visits <= v * 12:
            run(queue.pop(0))
    for unit in queue:
        run(unit)
    for j in range(R):
        if j not in ready:
            rest(j)
    for i in range(3, C - 1):
        def onward(c, i=i):
            for j in range(R):
                visit(i, j, c, True, go_right, go_left)

        loop(N, onward)
    for i in range(2, C - 1):
        @pl.when(from_left(i))
        def _(i=i):
            loop(N, lambda c: pieces(z - i, c))

        @pl.when(from_right(i))
        def _(i=i):
            loop(N, lambda c: pieces(z + i, c))

    @pl.when(is_last)
    def _():
        other = C - 1 - z

        def finish(c):
            for j in range(R):
                take(other, j, c)
            pieces(other, c)

        loop(N, finish)

    if lean:
        pl.when(is_end & (s == near_owner))(edge_pass)
        pl.when(takes_edge)(edge_place_all)

    for j in range(1, R):
        give_factor(j).wait_send()
    for j, k in straight:
        gather(0, j, k, j).wait_send()
    for j, k in by_way:
        relay(j, k)[1].wait_send()

    def drain(c):
        for j in range(R):
            @pl.when(own_right)
            def _(j=j):
                send_right(pbuf.at[z, j, rows(c)], z, j, c).wait_send()

            @pl.when(own_left)
            def _(j=j):
                send_left(pbuf.at[z, j, rows(c)], z, j, c).wait_send()

            for i in range(1, C - 1):
                @pl.when(from_left(i) & go_right)
                def _(i=i, j=j):
                    send_right(pbuf.at[z - i, j, rows(c)], z - i, j, c).wait_send()

                @pl.when(from_right(i) & go_left)
                def _(i=i, j=j):
                    send_left(pbuf.at[z + i, j, rows(c)], z + i, j, c).wait_send()

        for e in range(shares):
            @pl.when((share != e) & jnp.logical_not(takes_edge))
            def _(e=e):
                pltpu.make_async_copy(out.at[e, rows(c)], out.at[e, rows(c)], y_recv.at[e, c]).wait()

        for t in range(C):
            owner, place = target(t)
            used = jnp.logical_not(is_end & (near == t))

            @pl.when(used & (s != owner))
            def _(t=t):
                to_owner(t, c).wait_send()

            @pl.when(used & (s == owner) & (place != share))
            def _(t=t):
                to_row(t, c).wait_send()

    loop(N, drain)
    if lean:
        for h in range(strips):
            @pl.when(is_near & (s != edge_owner))
            def _(h=h):
                edge_to_owner(h).wait_send()

            @pl.when(is_near & (s == edge_owner))
            def _(h=h):
                edge_out(h).wait_send()

            @pl.when(is_end & (s == near_owner) & (near_place * blocks + h % blocks != r))
            def _(h=h):
                edge_to_row(h).wait_send()


def per_device(sizes, coeffs, occ_energy, vir_energy, frequency):
    S, R, C = sizes
    energy_gap = vir_energy[None, :] - occ_energy[:, None]
    factor = 2.0 * energy_gap / (energy_gap * energy_gap + frequency * frequency)
    occupied, local_vir, columns = coeffs.shape
    depth = occupied * local_vir
    blocks = S * R // C
    shares = R // blocks
    width = columns // R
    N = PIECES if width % (16 * PIECES) == 0 else 1
    sem = pltpu.SemaphoreType.DMA
    half, single = jnp.bfloat16, jnp.float32
    out = pl.pallas_call(
        functools.partial(response_kernel, S, R, C, N),
        out_shape=jax.ShapeDtypeStruct((shares, width, columns), jnp.float32),
        in_specs=[pl.BlockSpec(memory_space=pltpu.VMEM), pl.BlockSpec(memory_space=pl.ANY)],
        out_specs=pl.BlockSpec(memory_space=pltpu.VMEM),
        scratch_shapes=[
            pltpu.VMEM((depth, columns), half),
            pltpu.VMEM((8, depth), single),
            pltpu.VMEM((R, 8, depth), single),
            pltpu.VMEM((R, columns, depth), half),
            pltpu.VMEM((C, R, width, depth), half),
            pltpu.VMEM((width, depth), half),
            pltpu.VMEM((C, width, columns), single),
            pltpu.VMEM((shares, S - 1, width, columns), single),
            pltpu.VMEM((columns, width), single),
            pltpu.VMEM((S - 1, columns, width), single),
            pltpu.VMEM((columns, width), single),
            pltpu.VMEM((R, shares * width, width), single),
            sem((3,)), sem((R,)), sem((R,)), sem((R, R)), sem((R, R)), sem((2, C, R, N)), sem((C, R, N)),
            sem((C, N)), sem((shares, S - 1, N)), sem((C, N)), sem((shares, N)),
            sem((R,)), sem((S - 1, R)), sem((R,)), sem((R,)), sem((R,)), sem((R, shares)),
        ],
        compiler_params=pltpu.CompilerParams(collective_id=0, has_side_effects=True, vmem_limit_bytes=62 * 1024 * 1024),
        cost_estimate=pl.CostEstimate(flops=2 * C * R * width * depth * columns, bytes_accessed=8 * depth * columns, transcendentals=0),
    )(jnp.broadcast_to(factor.reshape(1, depth), (8, depth)), coeffs.reshape(depth, columns))
    return out.reshape(shares * width, columns)


def solution(mesh):
    placed = (P("section", "row", "col"), P("section"), P("row"), P())
    sizes = (mesh.shape["section"], mesh.shape["row"], mesh.shape["col"])
    return jax.shard_map(
        functools.partial(per_device, sizes),
        mesh=mesh,
        in_specs=placed,
        out_specs=P(("section", "row"), "col"),
        check_vma=False,
    )
```

```python
import functools

import jax
import jax.numpy as jnp
from jax import lax
from jax.experimental import pallas as pl
from jax.experimental.pallas import tpu as pltpu
from jax.sharding import PartitionSpec as P

MESH = pl.DeviceIdType.MESH


PIECES = 3


def response_kernel(S, R, C, N, factor, coeffs, out, raw, scale, fbuf, qbuf, pbuf, lbuf, tiles, parts, edge, edge_parts, edge_in, inbox,
                    loc_sem, fac_send, fac_recv, q_send, q_recv, p_send, p_recv, f_send, f_recv, y_send, y_recv,
                    e_send, e_recv, ez_send, ez_recv, ey_send, ey_recv):
    depth, columns = coeffs.shape
    width = columns // R
    blocks = S * R // C
    shares = R // blocks
    tall = shares * width
    piece = width // N
    lean = C >= 4
    step = columns // 3 if columns % 384 == 0 else columns
    s = lax.axis_index("section")
    r = lax.axis_index("row")
    z = lax.axis_index("col")
    share, half = r // blocks, r % blocks
    is_end = (z == 0) | (z == C - 1) if lean else z < 0
    is_near = (z == 1) | (z == C - 2) if lean else z < 0
    is_last = (z == 0) | (z == C - 1) if C > 2 else z < 0
    near = jnp.where(z == 0, 1, C - 2)
    end = jnp.where(z == 1, 0, C - 1)

    def peer(j):
        total, unit = 0, 1
        while unit < R:
            total = total + ((r // unit + j // unit) % 2) * unit
            unit *= 2
        return total

    def strip(row):
        first = ((row % blocks) * shares + row // blocks) * width
        return pl.ds(first if isinstance(row, int) else pl.multiple_of(first, width), width)

    def rows(c):
        return pl.ds(pl.multiple_of(c * piece, piece), piece)

    def loop(count, body):
        def run(n, carry):
            body(n)
            return carry

        lax.fori_loop(0, count, run, 0)

    def remote(source, there, sent, landed, **device):
        return pltpu.make_async_remote_copy(
            src_ref=source, dst_ref=there, send_sem=sent, recv_sem=landed, device_id=device, device_id_type=MESH)

    own = pltpu.make_async_copy(coeffs, raw, loc_sem.at[0])
    own.start()
    barrier = pltpu.get_barrier_semaphore()
    for j in range(1, R):
        pl.semaphore_signal(barrier, inc=1, device_id={"row": peer(j)}, device_id_type=MESH)
    for other in ((z + C - 1) % C, (z + 1) % C):
        pl.semaphore_signal(barrier, inc=1, device_id={"col": other}, device_id_type=MESH)
    for i in range(1, S):
        pl.semaphore_signal(barrier, inc=1, device_id={"section": (s + i) % S}, device_id_type=MESH)
    own.wait()
    chunk = min(256, depth)

    def turn(n):
        at = pl.ds(pl.multiple_of(n * chunk, chunk), chunk)
        qbuf[0, :, at] = raw[at, :].T

    loop(depth // chunk, turn)
    fbuf[0] = factor[...]
    pl.semaphore_wait(barrier, R + S)

    def give_factor(j):
        return remote(factor, fbuf.at[j], fac_send.at[j], fac_recv.at[j], row=peer(j))

    def gather(source, j, k, via):
        at = strip(peer(k))
        return remote(qbuf.at[source, at], qbuf.at[j, at], q_send.at[j, k], q_recv.at[j, k], row=peer(via))

    def landed(j, k):
        at = strip(peer(j ^ k))
        pltpu.make_async_copy(qbuf.at[j, at], qbuf.at[j, at], q_recv.at[j, k]).wait()

    direct = [j for j in range(1, R) if j & (j - 1) == 0]
    relayed = [j for j in range(1, R) if j & (j - 1)]

    def relay(j, k):
        low = j & -j
        via, kept = (low, j - low) if k % 2 else (j - low, low)
        at = strip(peer(via ^ j ^ k))
        return kept, remote(qbuf.at[kept, at], qbuf.at[j, at], q_send.at[j, k], q_recv.at[j, k], row=peer(via))

    def own_strip(j):
        return qbuf.at[j, strip(r)]

    def send_right(source, t, j, c):
        return remote(source, pbuf.at[t, j, rows(c)], p_send.at[0, t, j, c], p_recv.at[t, j, c], col=jnp.minimum(z + 1, C - 1))

    def send_left(source, t, j, c):
        return remote(source, pbuf.at[t, j, rows(c)], p_send.at[1, t, j, c], p_recv.at[t, j, c], col=jnp.maximum(z - 1, 0))

    own_right = (z < C - 1) & (z != C - 2) if lean else z < C - 1
    own_left = (z > 0) & (z != 1) if lean else z > 0

    def broadcast(j):
        def one(c):
            first = ((r % blocks) * shares + r // blocks) * width
            source = qbuf.at[j, pl.ds(pl.multiple_of(first + c * piece, piece), piece)]

            @pl.when(own_right)
            def _():
                send_right(source, z, j, c).start()

            @pl.when(own_left)
            def _():
                send_left(source, z, j, c).start()

        loop(N, one)

    for j in range(1, R):
        give_factor(j).start()
    arrived = set()

    def ensure(j, k):
        if (j, k) not in arrived:
            arrived.add((j, k))
            landed(j, k)

    by_way = [(j, k) for j in relayed for k in range(1, R) if k != j] if R == 4 else []
    straight = [(j, k) for j in range(1, R) for k in range(R) if (j, k) not in by_way]
    needed = [(relay(j, k)[0], k) for j, k in by_way]
    first = [(j, j) for j in direct]
    second_wave = [(j, j) for j in relayed]
    third = [pair for pair in needed if pair not in first]
    rest_wave = [pair for pair in straight if pair not in first + second_wave + third]

    def issue(pairs):
        for j, k in pairs:
            gather(0, j, k, j).start()

    issue(first)
    broadcast(0)
    for j in direct:
        ensure(j, j)
        if j == 1:
            issue(second_wave)
        broadcast(j)
    issue(third)
    for j in relayed:
        ensure(j, j)
        broadcast(j)
    for (j, k), pair in zip(by_way, needed):
        ensure(*pair)
        relay(j, k)[1].start()
    issue(rest_wave)

    def take(t, j, c):
        pltpu.make_async_copy(pbuf.at[t, j, rows(c)], pbuf.at[t, j, rows(c)], p_recv.at[t, j, c]).wait()

    def from_left(i):
        return (z >= i) & jnp.logical_not(is_end & (z == C - 1) & (i == 1)) if lean else z >= i

    def from_right(i):
        return (z + i < C) & jnp.logical_not(is_end & (z == 0) & (i == 1)) if lean else z + i < C

    def visit(i, j, c, wait, onward_right, onward_left):
        @pl.when(from_left(i))
        def _():
            if wait:
                take(z - i, j, c)

            @pl.when(onward_right)
            def _():
                send_right(pbuf.at[z - i, j, rows(c)], z - i, j, c).start()

        @pl.when(from_right(i))
        def _():
            if wait:
                take(z + i, j, c)

            @pl.when(onward_left)
            def _():
                send_left(pbuf.at[z + i, j, rows(c)], z + i, j, c).start()

    go_right, go_left = z < C - 1, z > 0
    for j in range(R):
        loop(N, lambda c, j=j: visit(1, j, c, True, go_right & jnp.logical_not(own_right), go_left & jnp.logical_not(own_left)))

    def second(c):
        for j in range(R):
            visit(1, j, c, False, go_right & own_right, go_left & own_left)

    loop(N, second)

    def times(value, j):
        return (value.astype(jnp.float32) * fbuf[j, 0:1, :]).astype(jnp.bfloat16)

    def dot(x, y):
        return lax.dot_general(x, y, (((1,), (1,)), ((), ())), preferred_element_type=jnp.float32)

    def product(t, load, at_rows, j):
        lbuf[at_rows, :] = times(load(), j)

        def body(n):
            at = pl.ds(pl.multiple_of(n * step, step), step)
            term = dot(lbuf[at_rows, :], qbuf[j, at, :])
            if j == 0:
                tiles[t, at_rows, at] = term
            else:
                tiles[t, at_rows, at] += term

        loop(columns // step, body)

    def target(t):
        return t // shares, t % shares

    def to_owner(t, c):
        owner, place = target(t)
        index = (s + S - owner + S - 1) % S
        return remote(tiles.at[t, rows(c)], parts.at[place, index, rows(c)], f_send.at[t, c], f_recv.at[place, index, c], section=owner)

    def to_row(t, c):
        return remote(tiles.at[t, rows(c)], out.at[share, rows(c)], y_send.at[t, c], y_recv.at[share, c], row=target(t)[1] * blocks + half)

    def hand_over(t, c):
        @pl.when(s != target(t)[0])
        def _():
            to_owner(t, c).start()

    def settle(t, c):
        owner, place = target(t)

        @pl.when(s == owner)
        def _():
            for i in range(S - 1):
                came = parts.at[place, i, rows(c)]
                pltpu.make_async_copy(came, came, f_recv.at[place, i, c]).wait()

            def add(n):
                at = pl.ds(pl.multiple_of(c * piece + n * 16, 16), 16)
                total = tiles[t, at, :]
                for i in range(S - 1):
                    total = total + parts[place, i, at, :]
                tiles[t, at, :] = total

            loop(piece // 16, add)

            @pl.when(place == share)
            def _():
                keep = pltpu.make_async_copy(tiles.at[t, rows(c)], out.at[share, rows(c)], loc_sem.at[1])
                keep.start()
                keep.wait()

            @pl.when(place != share)
            def _():
                to_row(t, c).start()

    edge_owner, edge_place = target(z)
    near_owner, near_place = target(near)

    strips = blocks * shares

    def edge_rows(h):
        return pl.ds(h % blocks * tall + h // blocks * width, width)

    def edge_to_owner(h):
        index = (s + S - edge_owner + S - 1) % S
        return remote(edge.at[edge_rows(h)], edge_parts.at[index, edge_rows(h)], e_send.at[h], e_recv.at[index, h], section=edge_owner)

    def edge_out(h):
        return remote(edge.at[edge_rows(h)], edge_in.at[edge_rows(h)], ez_send.at[h], ez_recv.at[h], col=end)

    def edge_to_row(h):
        e = h // blocks
        return remote(edge_in.at[edge_rows(h)], inbox.at[r, pl.ds(e * width, width)], ey_send.at[h], ey_recv.at[r, e], row=near_place * blocks + h % blocks)

    def edge_unit(j):
        def body(n):
            at = pl.ds(pl.multiple_of(n * step, step), step)
            term = dot(times(qbuf[j, at, :], j), pbuf[end, j])
            if j == 0:
                edge[at, :] = term
            else:
                edge[at, :] += term

        loop(columns // step, body)

    def edge_hand():
        @pl.when(s != edge_owner)
        def _():
            for h in range(strips):
                edge_to_owner(h).start()

    def edge_settle():
        @pl.when(s == edge_owner)
        def _():
            for h in range(strips):
                for i in range(S - 1):
                    came = edge_parts.at[i, edge_rows(h)]
                    pltpu.make_async_copy(came, came, e_recv.at[i, h]).wait()

                def add(n, h=h):
                    at = pl.ds(pl.multiple_of(h % blocks * tall + h // blocks * width + n * 16, 16), 16)
                    total = edge[at, :]
                    for i in range(S - 1):
                        total = total + edge_parts[i, at, :]
                    edge[at, :] = total

                loop(width // 16, add)
                edge_out(h).start()

    def edge_pass():
        for h in range(strips):
            came = edge_in.at[edge_rows(h)]
            pltpu.make_async_copy(came, came, ez_recv.at[h]).wait()
            goal = near_place * blocks + h % blocks

            @pl.when(goal != r)
            def _(h=h):
                edge_to_row(h).start()

            @pl.when(goal == r)
            def _(h=h):
                there = inbox.at[r, pl.ds(h // blocks * width, width)]
                keep = pltpu.make_async_copy(edge_in.at[edge_rows(h)], there, loc_sem.at[2])
                keep.start()
                keep.wait()

    takes_edge = is_end & (s == near_owner) & (share == near_place)

    def edge_place_all():
        first = [((row % blocks) * shares + row // blocks) * width for row in range(R)]
        for e in range(shares):
            for row in range(R):
                @pl.when(r != row)
                def _(row=row):
                    there = inbox.at[row, pl.ds(e * width, width)]
                    pltpu.make_async_copy(there, there, ey_recv.at[row, e]).wait()

                def put(n, row=row, e=e):
                    at = pl.ds(pl.multiple_of(n * 16, 16), 16)
                    out[e, at, first[row]:first[row] + width] = inbox[row, pl.ds(pl.multiple_of(e * width + n * 16, 16), 16), :]

                loop(width // 16, put)

    def rest(j):
        for k in range(R):
            if j:
                ensure(j, k)
        if j:
            give_factor(j).wait_recv()

    def pieces(t, c):
        for j in range(R):
            product(t, lambda j=j: pbuf[t, j, rows(c), :], rows(c), j)
        hand_over(t, c)
        settle(t, c)

    every = pl.ds(0, width)

    def own_unit(j):
        product(z, lambda: qbuf[j, strip(r), :], every, j)

    def left_unit(j):
        pl.when(from_left(1))(lambda: product(z - 1, lambda: pbuf[z - 1, j], every, j))

    def right_unit(j):
        pl.when(from_right(1))(lambda: product(z + 1, lambda: pbuf[z + 1, j], every, j))

    def near_unit(j):
        if lean:
            pl.when(is_near)(lambda: edge_unit(j))

    def near_step(work):
        if lean:
            pl.when(is_near)(work)

    def hand_all(t):
        loop(N, lambda c: hand_over(t, c))

    def settle_all(t):
        loop(N, lambda c: settle(t, c))

    def on_left(action):
        pl.when(from_left(1))(lambda: action(z - 1))

    def on_right(action):
        pl.when(from_right(1))(lambda: action(z + 1))

    later = 99
    units = [(0, own_unit, 0), (1, near_unit, 0), (2, left_unit, 0), (3, right_unit, 0)]
    units += [(7 + j, near_unit, j) for j in range(1, R)]
    units += [(10, lambda j: near_step(edge_hand), 0)]
    units += [(10, own_unit, 1), (10, lambda j: near_step(edge_settle), 0)]
    units += [(later, own_unit, j) for j in range(2, R)] + [(later, lambda j: hand_all(z), 0)]
    units += [(later, left_unit, j) for j in range(1, R)]
    units += [(later, lambda j: on_left(hand_all), 0), (later, lambda j: settle_all(z), 0)]
    units += [(later, right_unit, j) for j in range(1, R)]
    units += [(later, lambda j: on_right(hand_all), 0), (later, lambda j: on_left(settle_all), 0), (later, lambda j: on_right(settle_all), 0)]
    visits = N * R if C > 3 else 0
    ready = {0}

    def run(unit):
        when, work, j = unit
        if j not in ready:
            ready.add(j)
            rest(j)
        work(j)

    queue = list(units)
    for v in range(visits):
        visit(2, v % R, v // R, True, go_right, go_left)
        while queue and queue[0][0] * visits <= v * 12:
            run(queue.pop(0))
    for unit in queue:
        run(unit)
    for j in range(R):
        if j not in ready:
            rest(j)
    for i in range(3, C - 1):
        def onward(c, i=i):
            for j in range(R):
                visit(i, j, c, True, go_right, go_left)

        loop(N, onward)
    for i in range(2, C - 1):
        @pl.when(from_left(i))
        def _(i=i):
            loop(N, lambda c: pieces(z - i, c))

        @pl.when(from_right(i))
        def _(i=i):
            loop(N, lambda c: pieces(z + i, c))

    @pl.when(is_last)
    def _():
        other = C - 1 - z

        def finish(c):
            for j in range(R):
                take(other, j, c)
            pieces(other, c)

        loop(N, finish)

    if lean:
        pl.when(is_end & (s == near_owner))(edge_pass)
        pl.when(takes_edge)(edge_place_all)

    for j in range(1, R):
        give_factor(j).wait_send()
    for j, k in straight:
        gather(0, j, k, j).wait_send()
    for j, k in by_way:
        relay(j, k)[1].wait_send()

    def drain(c):
        for j in range(R):
            @pl.when(own_right)
            def _(j=j):
                send_right(pbuf.at[z, j, rows(c)], z, j, c).wait_send()

            @pl.when(own_left)
            def _(j=j):
                send_left(pbuf.at[z, j, rows(c)], z, j, c).wait_send()

            for i in range(1, C - 1):
                @pl.when(from_left(i) & go_right)
                def _(i=i, j=j):
                    send_right(pbuf.at[z - i, j, rows(c)], z - i, j, c).wait_send()

                @pl.when(from_right(i) & go_left)
                def _(i=i, j=j):
                    send_left(pbuf.at[z + i, j, rows(c)], z + i, j, c).wait_send()

        for e in range(shares):
            @pl.when((share != e) & jnp.logical_not(takes_edge))
            def _(e=e):
                pltpu.make_async_copy(out.at[e, rows(c)], out.at[e, rows(c)], y_recv.at[e, c]).wait()

        for t in range(C):
            owner, place = target(t)
            used = jnp.logical_not(is_end & (near == t))

            @pl.when(used & (s != owner))
            def _(t=t):
                to_owner(t, c).wait_send()

            @pl.when(used & (s == owner) & (place != share))
            def _(t=t):
                to_row(t, c).wait_send()

    loop(N, drain)
    if lean:
        for h in range(strips):
            @pl.when(is_near & (s != edge_owner))
            def _(h=h):
                edge_to_owner(h).wait_send()

            @pl.when(is_near & (s == edge_owner))
            def _(h=h):
                edge_out(h).wait_send()

            @pl.when(is_end & (s == near_owner) & (near_place * blocks + h % blocks != r))
            def _(h=h):
                edge_to_row(h).wait_send()


def per_device(sizes, coeffs, occ_energy, vir_energy, frequency):
    S, R, C = sizes
    energy_gap = vir_energy[None, :] - occ_energy[:, None]
    factor = 2.0 * energy_gap / (energy_gap * energy_gap + frequency * frequency)
    occupied, local_vir, columns = coeffs.shape
    depth = occupied * local_vir
    blocks = S * R // C
    shares = R // blocks
    width = columns // R
    N = PIECES if width % (16 * PIECES) == 0 else 1
    sem = pltpu.SemaphoreType.DMA
    half, single = jnp.bfloat16, jnp.float32
    out = pl.pallas_call(
        functools.partial(response_kernel, S, R, C, N),
        out_shape=jax.ShapeDtypeStruct((shares, width, columns), jnp.float32),
        in_specs=[pl.BlockSpec(memory_space=pltpu.VMEM), pl.BlockSpec(memory_space=pl.ANY)],
        out_specs=pl.BlockSpec(memory_space=pltpu.VMEM),
        scratch_shapes=[
            pltpu.VMEM((depth, columns), half),
            pltpu.VMEM((8, depth), single),
            pltpu.VMEM((R, 8, depth), single),
            pltpu.VMEM((R, columns, depth), half),
            pltpu.VMEM((C, R, width, depth), half),
            pltpu.VMEM((width, depth), half),
            pltpu.VMEM((C, width, columns), single),
            pltpu.VMEM((shares, S - 1, width, columns), single),
            pltpu.VMEM((columns, width), single),
            pltpu.VMEM((S - 1, columns, width), single),
            pltpu.VMEM((columns, width), single),
            pltpu.VMEM((R, shares * width, width), single),
            sem((3,)), sem((R,)), sem((R,)), sem((R, R)), sem((R, R)), sem((2, C, R, N)), sem((C, R, N)),
            sem((C, N)), sem((shares, S - 1, N)), sem((C, N)), sem((shares, N)),
            sem((R,)), sem((S - 1, R)), sem((R,)), sem((R,)), sem((R,)), sem((R, shares)),
        ],
        compiler_params=pltpu.CompilerParams(collective_id=0, has_side_effects=True, vmem_limit_bytes=62 * 1024 * 1024),
        cost_estimate=pl.CostEstimate(flops=2 * C * R * width * depth * columns, bytes_accessed=8 * depth * columns, transcendentals=0),
    )(jnp.broadcast_to(factor.reshape(1, depth), (8, depth)), coeffs.reshape(depth, columns))
    return out.reshape(shares * width, columns)


def solution(mesh):
    placed = (P("section", "row", "col"), P("section"), P("row"), P())
    sizes = (mesh.shape["section"], mesh.shape["row"], mesh.shape["col"])
    return jax.shard_map(
        functools.partial(per_device, sizes),
        mesh=mesh,
        in_specs=placed,
        out_specs=P(("section", "row"), "col"),
        check_vma=False,
    )
```

```python
import functools

import jax
import jax.numpy as jnp
from jax import lax
from jax.experimental import pallas as pl
from jax.experimental.pallas import tpu as pltpu
from jax.sharding import PartitionSpec as P

MESH = pl.DeviceIdType.MESH


PIECES = 3


def response_kernel(S, R, C, N, factor, coeffs, out, packed, pbuf, qbuf, tiles, parts, loc_sem, p_send, p_recv, a_send, q_send, q_recv, f_send, f_recv, y_send, y_recv):
    width, depth = packed.shape[1], packed.shape[2]
    columns = coeffs.shape[1]
    blocks = S * R // C
    shares = R // blocks
    piece = width // N
    step = columns // 3 if columns % 384 == 0 else columns
    s = lax.axis_index("section")
    r = lax.axis_index("row")
    z = lax.axis_index("col")
    share, half = r // blocks, r % blocks
    right, left = (z + 1) % C, (z + C - 1) % C

    def peer(j):
        total, unit = 0, 1
        while unit < R:
            total = total + ((r // unit + j // unit) % 2) * unit
            unit *= 2
        return total

    def rows(c):
        return pl.ds(pl.multiple_of(c * piece, piece), piece)

    own_q = pltpu.make_async_copy(coeffs, qbuf.at[0], loc_sem.at[0])
    own_q.start()
    barrier = pltpu.get_barrier_semaphore()
    for j in range(1, R):
        pl.semaphore_signal(barrier, inc=1, device_id={"row": peer(j)}, device_id_type=MESH)
    for other in (left, right):
        pl.semaphore_signal(barrier, inc=1, device_id={"col": other}, device_id_type=MESH)
    for i in range(1, S):
        pl.semaphore_signal(barrier, inc=1, device_id={"section": (s + i) % S}, device_id_type=MESH)

    def exchange(j, c):
        return pltpu.make_async_remote_copy(
            src_ref=packed.at[peer(j), rows(c)], dst_ref=pbuf.at[0, j, rows(c)], send_sem=a_send.at[j, c],
            recv_sem=p_recv.at[0, j, c], device_id={"row": peer(j)}, device_id_type=MESH)

    def gather(j):
        return pltpu.make_async_remote_copy(
            src_ref=coeffs, dst_ref=qbuf.at[j], send_sem=q_send.at[j], recv_sem=q_recv.at[j],
            device_id={"row": peer(j)}, device_id_type=MESH)

    def forward(t, j, c):
        return pltpu.make_async_remote_copy(
            src_ref=pbuf.at[t, j, rows(c)], dst_ref=pbuf.at[t + 1, j, rows(c)], send_sem=p_send.at[t, j, c],
            recv_sem=p_recv.at[t + 1, j, c], device_id={"col": right}, device_id_type=MESH)

    def loop(count, body):
        def run(n, carry):
            body(n)
            return carry

        lax.fori_loop(0, count, run, 0)

    own_q.wait()
    chunk = min(256, depth)
    for d in range(R):
        first = ((d % blocks) * shares + d // blocks) * width

        def pack(n, d=d, first=first):
            at = pl.ds(pl.multiple_of(n * chunk, chunk), chunk)
            value = qbuf[0, at, first:first + width].astype(jnp.float32) * factor[at, :]
            packed[d, :, at] = value.astype(jnp.bfloat16).T

        loop(depth // chunk, pack)
    own_p = pltpu.make_async_copy(packed.at[r], pbuf.at[0, 0], loc_sem.at[1])
    own_p.start()
    pl.semaphore_wait(barrier, R + S)

    def spread(c):
        for j in range(1, R):
            exchange(j, c).start()

    loop(N, spread)
    own_p.wait()
    forward(0, 0, 0).start()

    def begin(c):
        for j in range(1, R):
            exchange(j, c).wait_recv()
            forward(0, j, c).start()

    begin(0)
    for j in range(1, R):
        gather(j).start()

    def begin_next(c):
        forward(0, 0, c + 1).start()
        begin(c + 1)

    loop(N - 1, begin_next)
    for t in range(1, C - 1):

        def relay(c, t=t):
            for j in range(R):
                forward(t - 1, j, c).wait_recv()
                forward(t, j, c).start()

        loop(N, relay)

    def product(t, at_rows, j):
        def body(n):
            at = pl.ds(pl.multiple_of(n * step, step), step)
            term = jnp.dot(pbuf[t, j, at_rows, :], qbuf[j, :, at], preferred_element_type=jnp.float32)
            if j == 0:
                tiles[t, at_rows, at] = term
            else:
                tiles[t, at_rows, at] += term

        loop(columns // step, body)

    def target(t):
        origin = (z + C - t) % C
        return origin // shares, origin % shares

    def to_owner(t, c):
        owner, place = target(t)
        return pltpu.make_async_remote_copy(
            src_ref=tiles.at[t, rows(c)], dst_ref=parts.at[place, (s + S - owner) % S, rows(c)],
            send_sem=f_send.at[t, c], recv_sem=f_recv.at[place, (s + S - owner) % S, c],
            device_id={"section": owner}, device_id_type=MESH)

    def to_row(t, c):
        place = target(t)[1]
        return pltpu.make_async_remote_copy(
            src_ref=tiles.at[t, rows(c)], dst_ref=out.at[share, rows(c)], send_sem=y_send.at[t, c],
            recv_sem=y_recv.at[share, c], device_id={"row": place * blocks + half}, device_id_type=MESH)

    def hand_over(t, c):
        @pl.when(s != target(t)[0])
        def _():
            to_owner(t, c).start()

    def settle(t, c):
        owner, place = target(t)

        @pl.when(s == owner)
        def _():
            for i in range(1, S):
                arrived = parts.at[place, i, rows(c)]
                pltpu.make_async_copy(arrived, arrived, f_recv.at[place, i, c]).wait()

            def add(n):
                at = pl.ds(pl.multiple_of(c * piece + n * 16, 16), 16)
                total = tiles[t, at, :]
                for i in range(1, S):
                    total = total + parts[place, i, at, :]
                tiles[t, at, :] = total

            loop(piece // 16, add)

            @pl.when(place == share)
            def _():
                keep = pltpu.make_async_copy(tiles.at[t, rows(c)], out.at[share, rows(c)], loc_sem.at[2])
                keep.start()
                keep.wait()

            @pl.when(place != share)
            def _():
                to_row(t, c).start()

    for j in range(R):
        if j > 0:
            gather(j).wait_recv()
        loop(C - 1, lambda t, j=j: product(t, pl.ds(0, width), j))
    loop((C - 1) * N, lambda n: hand_over(n // N, n % N))
    loop((C - 1) * N, lambda n: settle(n // N, n % N))

    def finish(c):
        for j in range(R):
            forward(C - 2, j, c).wait_recv()
            product(C - 1, rows(c), j)
        hand_over(C - 1, c)
        settle(C - 1, c)

    loop(N, finish)

    def drain(c):
        for j in range(1, R):
            exchange(j, c).wait_send()
        for t in range(C - 1):
            for j in range(R):
                forward(t, j, c).wait_send()
        for e in range(shares):

            @pl.when(share != e)
            def _(e=e):
                pltpu.make_async_copy(out.at[e, rows(c)], out.at[e, rows(c)], y_recv.at[e, c]).wait()

    def drain_tiles(n):
        t, c = n // N, n % N
        owner, place = target(t)

        @pl.when(s != owner)
        def _():
            to_owner(t, c).wait_send()

        @pl.when((s == owner) & (place != share))
        def _():
            to_row(t, c).wait_send()

    for j in range(1, R):
        gather(j).wait_send()
    loop(C * N, drain_tiles)
    loop(N, drain)


def per_device(sizes, coeffs, occ_energy, vir_energy, frequency):
    S, R, C = sizes
    energy_gap = vir_energy[None, :] - occ_energy[:, None]
    factor = 2.0 * energy_gap / (energy_gap * energy_gap + frequency * frequency)
    occupied, local_vir, columns = coeffs.shape
    depth = occupied * local_vir
    blocks = S * R // C
    shares = R // blocks
    width = columns // R
    N = PIECES if width % (16 * PIECES) == 0 else 1
    sem = pltpu.SemaphoreType.DMA
    out = pl.pallas_call(
        functools.partial(response_kernel, S, R, C, N),
        out_shape=jax.ShapeDtypeStruct((shares, width, columns), jnp.float32),
        in_specs=[pl.BlockSpec(memory_space=pltpu.VMEM), pl.BlockSpec(memory_space=pl.ANY)],
        out_specs=pl.BlockSpec(memory_space=pltpu.VMEM),
        scratch_shapes=[
            pltpu.VMEM((R, width, depth), jnp.bfloat16),
            pltpu.VMEM((C, R, width, depth), jnp.bfloat16),
            pltpu.VMEM((R, depth, columns), jnp.bfloat16),
            pltpu.VMEM((C, width, columns), jnp.float32),
            pltpu.VMEM((shares, S, width, columns), jnp.float32),
            sem((3,)), sem((C, R, N)), sem((C, R, N)), sem((R, N)), sem((R,)), sem((R,)),
            sem((C, N)), sem((shares, S, N)), sem((C, N)), sem((shares, N)),
        ],
        compiler_params=pltpu.CompilerParams(collective_id=0, has_side_effects=True, vmem_limit_bytes=60 * 1024 * 1024),
        cost_estimate=pl.CostEstimate(flops=2 * C * R * width * depth * columns, bytes_accessed=8 * depth * columns, transcendentals=0),
    )(factor.reshape(depth, 1), coeffs.reshape(depth, columns))
    return out.reshape(shares * width, columns)


def solution(mesh):
    placed = (P("section", "row", "col"), P("section"), P("row"), P())
    sizes = (mesh.shape["section"], mesh.shape["row"], mesh.shape["col"])
    return jax.shard_map(
        functools.partial(per_device, sizes),
        mesh=mesh,
        in_specs=placed,
        out_specs=P(("section", "row"), "col"),
        check_vma=False,
    )
```
